32 devices in a mesh: groups: 2 (over y), span: 16 (over z, x, core).
Axes of the slice: x: 2, y: 2, z: 4, core: 2. Of those that a mesh axis runs over, the one named last changes fastest.
Arguments:
- queries: bfloat16 [8192, 3072], P(('groups', 'span')), parts along dimension 0, may hold values from -48 to 48
- keys: bfloat16 [8192, 1024], P(('groups', 'span')), parts along dimension 0, may hold values from -8 to 8
- values: bfloat16 [8192, 1024], P(('groups', 'span')), parts along dimension 0, may hold values from -6 to 6
- lookback: int32 [32], P(('groups', 'span')), parts along dimension 0, may hold values from 0 to 4, as said below
- w_out: bfloat16 [3072, 256], replicated, may hold values from -0.109375 to 0.109375
- conv_first: bfloat16 [3, 3, 3, 256, 256], replicated, may hold values from -0.078125 to 0.078125
- conv_second: bfloat16 [3, 3, 3, 256, 256], replicated, may hold values from -0.078125 to 0.078125
Outputs:
- decoded: bfloat16 [8192, 256], P(('groups', 'span')), parts along dimension 0
The draws below stay inside these ranges and needn't reach their ends.
There are 2 independent parts, one for each index of `groups`. The reference program is written for one: setup_inputs(seed, part) draws one part's arguments, and reference() takes and returns one part's arrays. A program takes and returns all parts, laid end to end along the dimension named above; an argument that names none is the same for every part. Nothing has to cross between parts.
Inputs may be any that keep to these rules, and one draw needn't show every extreme that they name: lookback[c] is at most c; the value 4 is reached in every draw.
All inputs are finite; a program needn't handle non-finite values.
Results may differ from the reference program's by a relative error of at most 0.007.
Values may be sent and summed in bfloat16 or wider, within the bound.
A program may use at most 64 MiB of HBM per device.

```python
import jax
import jax.numpy as jnp
from jax import lax

Q_HEADS = 24
KV_HEADS = 8
HEAD_DIM = 128
CHANNELS = 256
FRAMES = 4
ROWS = 8
COLS = 8
SPANS = 16
TOKENS = 4096


def query_key_pair(key):
    base = jax.random.fold_in(key, 17)
    first, second = jax.random.split(base, 2)
    ratio = Q_HEADS // KV_HEADS
    key_vecs = jnp.clip(jax.random.normal(first, (TOKENS, KV_HEADS, HEAD_DIM), jnp.float32), -6.0, 6.0)
    query_vecs = jnp.clip(jax.random.normal(second, (TOKENS, KV_HEADS, ratio, HEAD_DIM), jnp.float32), -6.0, 6.0)
    return (query_vecs.reshape(TOKENS, Q_HEADS * HEAD_DIM), key_vecs.reshape(TOKENS, KV_HEADS * HEAD_DIM))


def draw_queries(key, part):
    return query_key_pair(key)[0].astype(jnp.bfloat16)


def draw_keys(key, part):
    return query_key_pair(key)[1].astype(jnp.bfloat16)


def draw_lookback(key, part):
    reach = jax.random.randint(jax.random.fold_in(key, 5), (SPANS,), 1, 5)
    reach = reach.at[4].set(4)
    return jnp.minimum(reach, jnp.arange(SPANS)).astype(jnp.int32)


def block_levels(key, dims, shards, least, top_value):
    loudness = 1.0
    for dim, shards_of in shards:
        steps = jax.random.uniform(jax.random.fold_in(jax.random.fold_in(key, 6), dim), (shards_of,), jnp.float32, least / len(shards), top_value / len(shards))
        loudness = loudness * jnp.repeat(jnp.exp(steps), dims[dim] // shards_of).reshape((-1,) + (1,) * (len(dims) - 1 - dim))
    return loudness


def gaussian(rng, shape, spread, most, cuts=(), kind=jnp.bfloat16):
    entries = spread * jax.random.normal(rng, shape, jnp.float32)
    if cuts:
        entries = entries * block_levels(rng, shape, cuts, -0.22, 0.18)
    return jnp.clip(entries, -most, most).astype(kind)


def setup_inputs(seed: int = 0, part: int = 0) -> dict:
    splits = jax.random.split(jax.random.key(seed), 8)
    own_keys = jax.random.split(jax.random.fold_in(splits[7], part), 8)
    queries = draw_queries(jax.random.fold_in(jax.random.fold_in(splits[7], part), 71), part)
    keys = draw_keys(jax.random.fold_in(jax.random.fold_in(splits[7], part), 71), part)
    values = gaussian(own_keys[2], (TOKENS, KV_HEADS * HEAD_DIM), 1.0, 6.0, ((0, 16),))
    lookback = draw_lookback(jax.random.fold_in(jax.random.fold_in(splits[7], part), 71), part)
    w_out = gaussian(splits[4], (Q_HEADS * HEAD_DIM, CHANNELS), (Q_HEADS * HEAD_DIM) ** -0.5, 0.109375)
    conv_first = gaussian(splits[5], (3, 3, 3, CHANNELS, CHANNELS), (27 * CHANNELS) ** -0.5, 0.078125)
    conv_second = gaussian(splits[6], (3, 3, 3, CHANNELS, CHANNELS), (27 * CHANNELS) ** -0.5, 0.078125)
    return dict(queries=queries, keys=keys, values=values, lookback=lookback, w_out=w_out, conv_first=conv_first, conv_second=conv_second)


def attend(query_rows, key_rows, value_rows, visible):
    tok = query_rows.shape[0]
    groups = key_rows.shape[1] // HEAD_DIM
    ratio = query_rows.shape[1] // key_rows.shape[1]
    scale = 1.0 / jnp.sqrt(jnp.float32(HEAD_DIM))
    grouped = query_rows.reshape(tok, groups, ratio, HEAD_DIM)
    pieces = []
    for group in range(groups):
        qpart = grouped[:, group].astype(jnp.float32)
        kpart = key_rows[:, group * HEAD_DIM:(group + 1) * HEAD_DIM].astype(jnp.float32)
        vpart = value_rows[:, group * HEAD_DIM:(group + 1) * HEAD_DIM]
        scores = jnp.einsum('trd,sd->rts', qpart, kpart) * scale
        scores = jnp.where(visible[None, None, :], scores, -1e+30)
        peak = lax.optimization_barrier(jnp.max(scores, axis=-1, keepdims=True))
        weights = jnp.exp(scores - peak)
        total = lax.optimization_barrier(jnp.sum(weights, axis=-1))
        probs = weights.astype(jnp.bfloat16)
        mixed = jnp.einsum('rts,sd->rtd', probs.astype(jnp.float32), vpart.astype(jnp.float32)) / total[:, :, None]
        pieces.append(jnp.transpose(mixed, (1, 0, 2)).reshape(tok, ratio * HEAD_DIM))
    return jnp.concatenate(pieces, axis=-1).astype(jnp.bfloat16)

def conv_valid(extended, weight):
    frames_out = extended.shape[0] - 2
    rows = extended.shape[1]
    cols = extended.shape[2]
    chans = extended.shape[3]
    padded = jnp.pad(extended, ((0, 0), (1, 1), (1, 1), (0, 0)))
    columns = jnp.concatenate([padded[a:a + frames_out, b:b + rows, e:e + cols] for a in range(3) for b in range(3) for e in range(3)], axis=-1)
    columns = columns.reshape(frames_out * rows * cols, 27 * chans)
    return jnp.dot(columns, weight.reshape(27 * chans, weight.shape[4]), preferred_element_type=jnp.float32)

def reference(queries, keys, values, lookback, w_out, conv_first, conv_second):
    tok = FRAMES * ROWS * COLS
    spans = queries.shape[0] // tok
    width = keys.shape[1]
    key_pad = jnp.concatenate([jnp.zeros((4 * tok, width), jnp.bfloat16), keys], axis=0)
    value_pad = jnp.concatenate([jnp.zeros((4 * tok, width), jnp.bfloat16), values], axis=0)
    block = (jnp.arange(5 * tok) // tok).astype(jnp.int32)

    def one_span(index):
        start = (index * tok).astype(jnp.int32)
        query_rows = lax.dynamic_slice_in_dim(queries, start, tok, 0)
        key_rows = lax.dynamic_slice_in_dim(key_pad, start, 5 * tok, 0)
        value_rows = lax.dynamic_slice_in_dim(value_pad, start, 5 * tok, 0)
        visible = 4 - block <= lookback[index]
        attended = attend(query_rows, key_rows, value_rows, visible)
        return jnp.dot(attended, w_out, preferred_element_type=jnp.float32).astype(jnp.bfloat16)
    latent = lax.map(one_span, jnp.arange(spans, dtype=jnp.int32))
    chans = latent.shape[-1]
    latent = latent.reshape(spans * FRAMES, ROWS, COLS, chans)
    latent_pad = jnp.concatenate([jnp.zeros((2, ROWS, COLS, chans), jnp.bfloat16), latent], axis=0)

    def first_layer(index):
        window = lax.dynamic_slice_in_dim(latent_pad, (index * FRAMES).astype(jnp.int32), FRAMES + 2, 0)
        return jax.nn.silu(conv_valid(window, conv_first)).astype(jnp.bfloat16).reshape(FRAMES, ROWS, COLS, chans)
    hidden = lax.map(first_layer, jnp.arange(spans, dtype=jnp.int32)).reshape(spans * FRAMES, ROWS, COLS, chans)
    hidden_pad = jnp.concatenate([jnp.zeros((2, ROWS, COLS, chans), jnp.bfloat16), hidden], axis=0)

    def second_layer(index):
        window = lax.dynamic_slice_in_dim(hidden_pad, (index * FRAMES).astype(jnp.int32), FRAMES + 2, 0)
        return conv_valid(window, conv_second).astype(jnp.bfloat16)
    decoded = lax.map(second_layer, jnp.arange(spans, dtype=jnp.int32))
    return decoded.reshape(spans * tok, chans)
```

```python
import functools

import jax
import jax.numpy as jnp
from jax import lax
from jax.experimental import pallas as pl
from jax.experimental.pallas import tpu as pltpu
from jax.sharding import PartitionSpec as P

HEAD_DIM = 128
FRAMES = 4
ROWS = 8
COLS = 8
REACH = 4
LOG2E = 1.4426950408889634
MESH = pl.DeviceIdType.MESH
DOT_T = (((1,), (1,)), ((), ()))


def kernel(n, q_hbm, k_hbm, v_hbm, look, w_hbm, c1_hbm, c2_hbm, out,
           q, kv, w, c1, c2, acc, halo_out, halo_in, ext,
           kv_sem, q_sem, w_sem, send, recv, halo_send, halo_recv):
    me = lax.axis_index("span")
    core = lax.rem(me, 2)
    side = lax.rem(me // 2, 2)
    groups = kv.shape[1]
    tok = q.shape[1]
    chans = acc.shape[1]
    wide = q.shape[2]
    ratio = wide // HEAD_DIM
    area = ROWS * COLS
    partner = me + 1 - 2 * core
    across = me + 2 - 4 * side

    def local_kv(g, half):
        src = (k_hbm, v_hbm)[half]
        cols = pl.ds(g * HEAD_DIM, HEAD_DIM)
        return pltpu.make_async_copy(src.at[:, cols], kv.at[0, g, half], kv_sem.at[g, half])

    def local_q(g):
        start = g * wide if isinstance(g, int) else pl.multiple_of(g * wide, wide)
        return pltpu.make_async_copy(q_hbm.at[:, pl.ds(start, wide)], q.at[g], q_sem.at[g])

    weights = [
        pltpu.make_async_copy(src, dst, w_sem.at[i])
        for i, (src, dst) in enumerate(((w_hbm, w), (c1_hbm, c1), (c2_hbm, c2)))
    ]

    def remote(src_slot, dst_slot, g, lane, target):
        return pltpu.make_async_remote_copy(
            src_ref=kv.at[src_slot, g],
            dst_ref=kv.at[dst_slot, g],
            send_sem=send.at[lane, g],
            recv_sem=recv.at[dst_slot, g],
            device_id={"span": target},
            device_id_type=MESH,
        )

    def arrived(slot, g):
        remote(slot, slot, g, 0, partner).wait_recv()

    for g in range(groups):
        for half in range(2):
            local_kv(g, half).start()
    for g in range(groups):
        local_q(g).start()
    for copy in weights:
        copy.start()

    barrier = pltpu.get_barrier_semaphore()
    near = (
        (me >= 4, me - 4),
        (me + 4 < n, me + 4),
        (me >= 1, me - 1),
        (me + 1 < n, me + 1),
        (me >= 0, across),
    )
    for there, target in near:
        @pl.when(there)
        def _():
            pl.semaphore_signal(barrier, inc=1, device_id={"span": target}, device_id_type=MESH)
    count = sum(jnp.where(there, 1, 0).astype(jnp.int32) for there, _unused in near)
    pl.semaphore_wait(barrier, count)

    @pl.loop(0, groups)
    def _(g):
        for half in range(2):
            pltpu.make_async_copy(
                k_hbm.at[:, pl.ds(0, HEAD_DIM)], kv.at[0, g, half], kv_sem.at[g, half]
            ).wait()

        @pl.when(me + 4 < n)
        def _():
            remote(0, 4, g, 0, me + 4).start()

        @pl.when(side == 0)
        def _():
            remote(0, 2, g, 1, across).start()

        @pl.when(core == 0)
        def _():
            remote(0, 1, g, 2, partner).start()

    for slot in range(1, REACH + 1):
        @pl.when(me < slot)
        def _():
            kv[slot] = jnp.zeros(kv.shape[1:], kv.dtype)

    weights[0].wait()
    acc[...] = jnp.zeros_like(acc)
    bias = [jnp.where(j <= look[0], 0.0, 1e30).astype(jnp.float32) for j in range(REACH + 1)]
    factor = LOG2E / HEAD_DIM**0.5
    ones = jnp.ones((tok, HEAD_DIM), jnp.bfloat16)

    def attend(g):
        heads = []
        for r in range(ratio):
            query = q[g, :, r * HEAD_DIM : (r + 1) * HEAD_DIM]
            scores = []
            top = None
            for j in range(REACH + 1):
                s = lax.dot_general(query, kv[j, g, 0], DOT_T, preferred_element_type=jnp.float32)
                scores.append(s)
                peak = s[:, :HEAD_DIM]
                for start in range(HEAD_DIM, tok, HEAD_DIM):
                    peak = jnp.maximum(peak, s[:, start : start + HEAD_DIM])
                peak = peak - bias[j]
                top = peak if top is None else jnp.maximum(top, peak)
            top = jnp.max(top, axis=1, keepdims=True)
            mixed = None
            for j in range(REACH + 1):
                probs = jnp.exp2((scores[j] - (top + bias[j])) * factor).astype(jnp.bfloat16)
                vals = jnp.concatenate([kv[j, g, 1], ones], axis=1)
                part = jnp.dot(probs, vals, preferred_element_type=jnp.float32)
                mixed = part if mixed is None else mixed + part
            heads.append((mixed[:, :HEAD_DIM] / mixed[:, HEAD_DIM:]).astype(jnp.bfloat16))
        attended = jnp.concatenate(heads, axis=1)
        rows = pl.ds(pl.multiple_of(g * wide, wide), wide)
        acc[...] += jnp.dot(attended, w[rows, :], preferred_element_type=jnp.float32)

    @pl.loop(0, groups + 2)
    def _(t):
        @pl.when((t < groups) & (me >= 4))
        def _():
            arrived(4, t)

            @pl.when(side == 1)
            def _():
                remote(4, 2, t, 1, across).start()

            @pl.when(core == 1)
            def _():
                remote(4, 3, t, 2, partner).start()

        @pl.when((t >= 1) & (t <= groups) & (me >= 2))
        def _():
            arrived(2, t - 1)

            @pl.when(core == 0)
            def _():
                remote(2, 3, t - 1, 3, partner).start()

            @pl.when(core == 1)
            def _():
                remote(2, 1, t - 1, 3, partner).start()

        @pl.when(t >= 2)
        def _():
            g = t - 2

            @pl.when(me >= 1)
            def _():
                arrived(1, g)

            @pl.when(me >= 3)
            def _():
                arrived(3, g)

            local_q(g).wait()
            attend(g)

    frame = lax.broadcasted_iota(jnp.int32, (2 * area, chans), 0)
    column = lax.rem(frame, COLS)

    def halo(which):
        return pltpu.make_async_remote_copy(
            src_ref=halo_out.at[which],
            dst_ref=halo_in.at[which],
            send_sem=halo_send.at[which],
            recv_sem=halo_recv.at[which],
            device_id={"span": lax.rem(me + 1, n)},
            device_id_type=MESH,
        )

    def place(layer, first, x):
        shifted = (
            jnp.where(column == 0, 0.0, pltpu.roll(x, 1, 0)),
            x,
            jnp.where(column == COLS - 1, 0.0, pltpu.roll(x, 2 * area - 1, 0)),
        )
        for e in range(3):
            for f in range(2):
                ext[layer, e, first + f, COLS : COLS + area, :] = shifted[e][f * area : (f + 1) * area]

    def conv(layer, weight, first):
        total = None
        for a in range(3):
            taps = []
            for b in range(3):
                for e in range(3):
                    taps.append(jnp.concatenate(
                        [
                            ext[layer, e, first + f + a, b * COLS : b * COLS + area, :]
                            for f in range(2)
                        ], axis=0).astype(jnp.bfloat16))
            part = jnp.dot(
                jnp.concatenate(taps, axis=1),
                weight[a * 9 * chans : (a + 1) * 9 * chans, :],
                preferred_element_type=jnp.float32,
            )
            total = part if total is None else total + part
        return total

    edge = jnp.zeros((2, 3, FRAMES + 2, COLS, chans), jnp.float32)
    ext[:, :, :, :COLS, :] = edge
    ext[:, :, :, COLS + area :, :] = edge

    def send_halo(which, x):
        halo_out[which] = x

        @pl.when(me + 1 < n)
        def _():
            halo(which).start()

    def receive_halo(which):
        @pl.when(me == 0)
        def _():
            halo_in[which] = jnp.zeros(halo_in.shape[1:], halo_in.dtype)

        @pl.when(me >= 1)
        def _():
            halo(which).wait_recv()

        place(which, 0, halo_in[which].astype(jnp.float32))

    half = 2 * area
    latent = acc[half:, :].astype(jnp.bfloat16)
    send_halo(0, latent)
    place(0, 4, latent.astype(jnp.float32))
    place(0, 2, acc[:half, :].astype(jnp.bfloat16).astype(jnp.float32))
    weights[1].wait()
    hidden = jax.nn.silu(conv(0, c1, 2)).astype(jnp.bfloat16)
    send_halo(1, hidden)
    place(1, 4, hidden.astype(jnp.float32))
    receive_halo(0)
    hidden = jax.nn.silu(conv(0, c1, 0)).astype(jnp.bfloat16)
    place(1, 2, hidden.astype(jnp.float32))
    weights[2].wait()
    out[half:, :] = conv(1, c2, 2).astype(out.dtype)
    receive_halo(1)
    out[:half, :] = conv(1, c2, 0).astype(out.dtype)

    @pl.when(me + 1 < n)
    def _():
        for which in range(2):
            halo(which).wait_send()

    @pl.loop(0, groups)
    def _(g):
        @pl.when(me + 4 < n)
        def _():
            remote(0, 4, g, 0, partner).wait_send()

        @pl.when((side == 0) | (me >= 4))
        def _():
            remote(0, 2, g, 1, partner).wait_send()

        @pl.when((core == 0) | (me >= 4))
        def _():
            remote(0, 1, g, 2, partner).wait_send()

        @pl.when(me >= 2)
        def _():
            remote(2, 3, g, 3, partner).wait_send()


def on_device(n, queries, keys, values, lookback, w_out, conv_first, conv_second):
    tok = queries.shape[0]
    chans = w_out.shape[1]
    groups = keys.shape[1] // HEAD_DIM
    wide = queries.shape[1] // groups
    taps = 27 * chans
    area = ROWS * COLS
    hbm = pl.BlockSpec(memory_space=pltpu.HBM)
    bf16 = jnp.bfloat16
    dma = pltpu.SemaphoreType.DMA
    return pl.pallas_call(
        functools.partial(kernel, n),
        out_shape=jax.ShapeDtypeStruct((tok, chans), bf16),
        in_specs=[hbm, hbm, hbm, pl.BlockSpec(memory_space=pltpu.SMEM), hbm, hbm, hbm],
        out_specs=pl.BlockSpec(memory_space=pltpu.VMEM),
        scratch_shapes=[
            pltpu.VMEM((groups, tok, wide), bf16),
            pltpu.VMEM((REACH + 1, groups, 2, tok, HEAD_DIM), bf16),
            pltpu.VMEM(w_out.shape, bf16),
            pltpu.VMEM((taps, chans), bf16),
            pltpu.VMEM((taps, chans), bf16),
            pltpu.VMEM((tok, chans), jnp.float32),
            pltpu.VMEM((2, 2 * area, chans), bf16),
            pltpu.VMEM((2, 2 * area, chans), bf16),
            pltpu.VMEM((2, 3, FRAMES + 2, area + 2 * COLS, chans), jnp.float32),
            dma((groups, 2)),
            dma((groups,)),
            dma((3,)),
            dma((4, groups)),
            dma((REACH + 1, groups)),
            dma((2,)),
            dma((2,)),
        ],
        compiler_params=pltpu.CompilerParams(
            collective_id=0, has_side_effects=True, vmem_limit_bytes=56 * 1024 * 1024
        ),
    )(
        queries, keys, values, lookback, w_out,
        conv_first.reshape(taps, chans), conv_second.reshape(taps, chans),
    )


def solution(mesh):
    placed = (
        P(("groups", "span"), None),
        P(("groups", "span"), None),
        P(("groups", "span"), None),
        P(("groups", "span")),
        P(),
        P(),
        P(),
    )
    return jax.shard_map(
        functools.partial(on_device, mesh.shape["span"]),
        mesh=mesh,
        in_specs=placed,
        out_specs=P(("groups", "span"), None),
        check_vma=False,
    )
```

```python
import functools

import jax
import jax.numpy as jnp
from jax import lax
from jax.experimental import pallas as pl
from jax.experimental.pallas import tpu as pltpu
from jax.sharding import PartitionSpec as P

HEAD_DIM = 128
FRAMES = 4
ROWS = 8
COLS = 8
REACH = 4
LOG2E = 1.4426950408889634
MESH = pl.DeviceIdType.MESH
DOT_T = (((1,), (1,)), ((), ()))


def kernel(n, q_hbm, k_hbm, v_hbm, look, w_hbm, c1_hbm, c2_hbm, out,
           q, kv, w, c1, c2, acc, halo_out, halo_in, ext,
           kv_sem, q_sem, w_sem, send, recv, halo_send, halo_recv):
    me = lax.axis_index("span")
    core = lax.rem(me, 2)
    side = lax.rem(me // 2, 2)
    groups = kv.shape[1]
    tok = q.shape[1]
    chans = acc.shape[1]
    wide = q.shape[2]
    ratio = wide // HEAD_DIM
    area = ROWS * COLS
    partner = me + 1 - 2 * core
    across = me + 2 - 4 * side

    def local_kv(g, half):
        src = (k_hbm, v_hbm)[half]
        cols = pl.ds(g * HEAD_DIM, HEAD_DIM)
        return pltpu.make_async_copy(src.at[:, cols], kv.at[0, g, half], kv_sem.at[g, half])

    def local_q(g):
        start = g * wide if isinstance(g, int) else pl.multiple_of(g * wide, wide)
        return pltpu.make_async_copy(q_hbm.at[:, pl.ds(start, wide)], q.at[g], q_sem.at[g])

    weights = [
        pltpu.make_async_copy(src, dst, w_sem.at[i])
        for i, (src, dst) in enumerate(((w_hbm, w), (c1_hbm, c1), (c2_hbm, c2)))
    ]

    def remote(src_slot, dst_slot, g, lane, target):
        return pltpu.make_async_remote_copy(
            src_ref=kv.at[src_slot, g],
            dst_ref=kv.at[dst_slot, g],
            send_sem=send.at[lane, g],
            recv_sem=recv.at[dst_slot, g],
            device_id={"span": target},
            device_id_type=MESH,
        )

    def arrived(slot, g):
        remote(slot, slot, g, 0, partner).wait_recv()

    for g in range(groups):
        for half in range(2):
            local_kv(g, half).start()
    for g in range(groups):
        local_q(g).start()
    for copy in weights:
        copy.start()

    barrier = pltpu.get_barrier_semaphore()
    near = (
        (me >= 4, me - 4),
        (me + 4 < n, me + 4),
        (me >= 1, me - 1),
        (me + 1 < n, me + 1),
        (me >= 0, across),
    )
    for there, target in near:
        @pl.when(there)
        def _():
            pl.semaphore_signal(barrier, inc=1, device_id={"span": target}, device_id_type=MESH)
    count = sum(jnp.where(there, 1, 0).astype(jnp.int32) for there, _unused in near)
    pl.semaphore_wait(barrier, count)

    @pl.loop(0, groups)
    def _(g):
        for half in range(2):
            pltpu.make_async_copy(
                k_hbm.at[:, pl.ds(0, HEAD_DIM)], kv.at[0, g, half], kv_sem.at[g, half]
            ).wait()

        @pl.when(me + 4 < n)
        def _():
            remote(0, 4, g, 0, me + 4).start()

        @pl.when(side == 0)
        def _():
            remote(0, 2, g, 1, across).start()

        @pl.when(core == 0)
        def _():
            remote(0, 1, g, 2, partner).start()

    for slot in range(1, REACH + 1):
        @pl.when(me < slot)
        def _():
            kv[slot] = jnp.zeros(kv.shape[1:], kv.dtype)

    weights[0].wait()
    acc[...] = jnp.zeros_like(acc)
    bias = [jnp.where(j <= look[0], 0.0, 1e30).astype(jnp.float32) for j in range(REACH + 1)]
    factor = LOG2E / HEAD_DIM**0.5
    ones = jnp.ones((tok, HEAD_DIM), jnp.bfloat16)

    def attend(g):
        heads = []
        for r in range(ratio):
            query = q[g, :, r * HEAD_DIM : (r + 1) * HEAD_DIM]
            scores = []
            top = None
            for j in range(REACH + 1):
                s = lax.dot_general(query, kv[j, g, 0], DOT_T, preferred_element_type=jnp.float32)
                scores.append(s)
                peak = s[:, :HEAD_DIM]
                for start in range(HEAD_DIM, tok, HEAD_DIM):
                    peak = jnp.maximum(peak, s[:, start : start + HEAD_DIM])
                peak = peak - bias[j]
                top = peak if top is None else jnp.maximum(top, peak)
            top = jnp.max(top, axis=1, keepdims=True)
            mixed = None
            for j in range(REACH + 1):
                probs = jnp.exp2((scores[j] - (top + bias[j])) * factor).astype(jnp.bfloat16)
                vals = jnp.concatenate([kv[j, g, 1], ones], axis=1)
                part = jnp.dot(probs, vals, preferred_element_type=jnp.float32)
                mixed = part if mixed is None else mixed + part
            heads.append((mixed[:, :HEAD_DIM] / mixed[:, HEAD_DIM:]).astype(jnp.bfloat16))
        attended = jnp.concatenate(heads, axis=1)
        rows = pl.ds(pl.multiple_of(g * wide, wide), wide)
        acc[...] += jnp.dot(attended, w[rows, :], preferred_element_type=jnp.float32)

    @pl.loop(0, groups + 2)
    def _(t):
        @pl.when((t < groups) & (me >= 4))
        def _():
            arrived(4, t)

            @pl.when(side == 1)
            def _():
                remote(4, 2, t, 1, across).start()

            @pl.when(core == 1)
            def _():
                remote(4, 3, t, 2, partner).start()

        @pl.when((t >= 1) & (t <= groups) & (me >= 2))
        def _():
            arrived(2, t - 1)

            @pl.when(core == 0)
            def _():
                remote(2, 3, t - 1, 3, partner).start()

            @pl.when(core == 1)
            def _():
                remote(2, 1, t - 1, 3, partner).start()

        @pl.when(t >= 2)
        def _():
            g = t - 2

            @pl.when(me >= 1)
            def _():
                arrived(1, g)

            @pl.when(me >= 3)
            def _():
                arrived(3, g)

            local_q(g).wait()
            attend(g)

    frame = lax.broadcasted_iota(jnp.int32, (2 * area, chans), 0)
    column = lax.rem(frame, COLS)

    def halo(which):
        return pltpu.make_async_remote_copy(
            src_ref=halo_out.at[which],
            dst_ref=halo_in.at[which],
            send_sem=halo_send.at[which],
            recv_sem=halo_recv.at[which],
            device_id={"span": lax.rem(me + 1, n)},
            device_id_type=MESH,
        )

    def place(layer, first, x):
        shifted = (
            jnp.where(column == 0, 0.0, pltpu.roll(x, 1, 0)),
            x,
            jnp.where(column == COLS - 1, 0.0, pltpu.roll(x, 2 * area - 1, 0)),
        )
        for e in range(3):
            for f in range(2):
                ext[layer, e, first + f, COLS : COLS + area, :] = shifted[e][f * area : (f + 1) * area]

    def conv(layer, weight, first):
        total = None
        for a in range(3):
            taps = []
            for b in range(3):
                for e in range(3):
                    taps.append(jnp.concatenate(
                        [
                            ext[layer, e, first + f + a, b * COLS : b * COLS + area, :]
                            for f in range(2)
                        ], axis=0).astype(jnp.bfloat16))
            part = jnp.dot(
                jnp.concatenate(taps, axis=1),
                weight[a * 9 * chans : (a + 1) * 9 * chans, :],
                preferred_element_type=jnp.float32,
            )
            total = part if total is None else total + part
        return total

    edge = jnp.zeros((2, 3, FRAMES + 2, COLS, chans), jnp.float32)
    ext[:, :, :, :COLS, :] = edge
    ext[:, :, :, COLS + area :, :] = edge

    def send_halo(which, x):
        halo_out[which] = x

        @pl.when(me + 1 < n)
        def _():
            halo(which).start()

    def receive_halo(which):
        @pl.when(me == 0)
        def _():
            halo_in[which] = jnp.zeros(halo_in.shape[1:], halo_in.dtype)

        @pl.when(me >= 1)
        def _():
            halo(which).wait_recv()

        place(which, 0, halo_in[which].astype(jnp.float32))

    half = 2 * area
    latent = acc[half:, :].astype(jnp.bfloat16)
    send_halo(0, latent)
    place(0, 4, latent.astype(jnp.float32))
    place(0, 2, acc[:half, :].astype(jnp.bfloat16).astype(jnp.float32))
    weights[1].wait()
    hidden = jax.nn.silu(conv(0, c1, 2)).astype(jnp.bfloat16)
    send_halo(1, hidden)
    place(1, 4, hidden.astype(jnp.float32))
    receive_halo(0)
    hidden = jax.nn.silu(conv(0, c1, 0)).astype(jnp.bfloat16)
    place(1, 2, hidden.astype(jnp.float32))
    weights[2].wait()
    out[half:, :] = conv(1, c2, 2).astype(out.dtype)
    receive_halo(1)
    out[:half, :] = conv(1, c2, 0).astype(out.dtype)

    @pl.when(me + 1 < n)
    def _():
        for which in range(2):
            halo(which).wait_send()

    @pl.loop(0, groups)
    def _(g):
        @pl.when(me + 4 < n)
        def _():
            remote(0, 4, g, 0, partner).wait_send()

        @pl.when((side == 0) | (me >= 4))
        def _():
            remote(0, 2, g, 1, partner).wait_send()

        @pl.when((core == 0) | (me >= 4))
        def _():
            remote(0, 1, g, 2, partner).wait_send()

        @pl.when(me >= 2)
        def _():
            remote(2, 3, g, 3, partner).wait_send()


def on_device(n, queries, keys, values, lookback, w_out, conv_first, conv_second):
    tok = queries.shape[0]
    chans = w_out.shape[1]
    groups = keys.shape[1] // HEAD_DIM
    wide = queries.shape[1] // groups
    taps = 27 * chans
    area = ROWS * COLS
    hbm = pl.BlockSpec(memory_space=pltpu.HBM)
    bf16 = jnp.bfloat16
    dma = pltpu.SemaphoreType.DMA
    return pl.pallas_call(
        functools.partial(kernel, n),
        out_shape=pltpu.VMEM((tok, chans), bf16),
        in_specs=[hbm, hbm, hbm, pl.BlockSpec(memory_space=pltpu.SMEM), hbm, hbm, hbm],
        out_specs=pl.BlockSpec(memory_space=pltpu.VMEM),
        scratch_shapes=[
            pltpu.VMEM((groups, tok, wide), bf16),
            pltpu.VMEM((REACH + 1, groups, 2, tok, HEAD_DIM), bf16),
            pltpu.VMEM(w_out.shape, bf16),
            pltpu.VMEM((taps, chans), bf16),
            pltpu.VMEM((taps, chans), bf16),
            pltpu.VMEM((tok, chans), jnp.float32),
            pltpu.VMEM((2, 2 * area, chans), bf16),
            pltpu.VMEM((2, 2 * area, chans), bf16),
            pltpu.VMEM((2, 3, FRAMES + 2, area + 2 * COLS, chans), jnp.float32),
            dma((groups, 2)),
            dma((groups,)),
            dma((3,)),
            dma((4, groups)),
            dma((REACH + 1, groups)),
            dma((2,)),
            dma((2,)),
        ],
        compiler_params=pltpu.CompilerParams(
            collective_id=0, has_side_effects=True, vmem_limit_bytes=56 * 1024 * 1024
        ),
    )(
        queries, keys, values, lookback, w_out,
        conv_first.reshape(taps, chans), conv_second.reshape(taps, chans),
    )


def solution(mesh):
    placed = (
        P(("groups", "span"), None),
        P(("groups", "span"), None),
        P(("groups", "span"), None),
        P(("groups", "span")),
        P(),
        P(),
        P(),
    )
    return jax.shard_map(
        functools.partial(on_device, mesh.shape["span"]),
        mesh=mesh,
        in_specs=placed,
        out_specs=P(("groups", "span"), None),
        check_vma=False,
    )
```
